512 devices in a mesh: dp: 64 (over z, y), seq: 8 (over x, core).
Axes of the slice: x: 4, y: 4, z: 16, core: 2. Of those that a mesh axis runs over, the one named last changes fastest.
Arguments:
- token_rows: bfloat16 [65536, 4096], P(('dp', 'seq')), may hold values from -16 to 16
- extra_len: int32 [64, 16], P('dp'), may hold values from 1 to 497, 784 in all within a row
- queries: bfloat16 [1024, 4096], P(('dp', 'seq')), may hold values from -8 to 8
- positive: int32 [1024], replicated, may hold values from 0 to 1023
Outputs:
- grad_rows: bfloat16 [65536, 4096], P(('dp', 'seq'))
The draws below stay inside these ranges and needn't reach their ends.
Inputs may be any that keep to these rules, and one draw needn't show every extreme that they name: `extra_len`: each group's entries sum to 784, and in every group one passage has 512 tokens.
All inputs are finite; a program needn't handle non-finite values.
Results may differ from the reference program's by a relative error of at most 0.0053.
Values may be sent and summed in bfloat16 or wider, within the bound.
No kernel may reach another device: no remote copies, remote signals or barrier semaphores. Data moves between devices by JAX's collectives and lax.ppermute only.
A program may use at most 64 MiB of HBM per device.

```python
import math
import jax
import jax.numpy as jnp
import numpy as np
from jax import lax

D = 4096
ROWS_G = 1024
PASS_G = 16
LONGEST = 512
GROUPS = 64
PASSAGES = 1024
TOKENS = 65536
QUERIES = 1024


def block_directions(key):
    return jax.random.normal(key, (TOKENS // 64, D), jnp.float32)


def draw_token_rows(key, part):
    directions = block_directions(key)
    key = jax.random.fold_in(key, 7)
    noise_key = jax.random.fold_in(key, 0)
    noise = jax.random.normal(noise_key, (TOKENS, D), jnp.float32)
    values = noise + jnp.repeat(directions, 64, axis=0)
    return jnp.clip(values, -16.0, 16.0).astype(jnp.bfloat16)


def draw_queries(key, part):
    directions = block_directions(key)
    key = jax.random.fold_in(key, 9)
    pick_key, noise_key = jax.random.split(key)
    picks = jax.random.randint(pick_key, (QUERIES,), 0, TOKENS // 64)
    noise = 0.3 * jax.random.normal(noise_key, (QUERIES, D), jnp.float32)
    values = directions[picks] + noise
    return jnp.clip(values, -8.0, 8.0).astype(jnp.bfloat16)


def set_ends(array, stream_key, smallest, largest):
    spot = [jax.random.randint(jax.random.fold_in(stream_key, axis), (), 0, length) for axis, length in enumerate(array.shape)]
    longest = array.shape.index(max(array.shape))
    beside = spot[:longest] + [(spot[longest] + 1) % array.shape[longest]] + spot[longest + 1:]
    return array.at[tuple(spot)].set(smallest).at[tuple(beside)].set(largest)


def profile(amount, total, limit, lean):
    weights = [(1 << 20) // math.isqrt(grade ** lean) + 1 for grade in range(2, amount + 1)]
    surplus, given = total - limit - (amount - 1), [1] * (amount - 1)
    while surplus > 0:
        free = [i for i in range(amount - 1) if given[i] < limit]
        mass, budget = sum([weights[i] for i in free]), surplus
        for i in free:
            extra = min(limit - given[i], max(1, budget * weights[i] // mass), surplus)
            given[i] = given[i] + extra
            surplus = surplus - extra
    return np.array([limit] + given)


def ragged_sizes(key, amount, total, bound, lean):
    if amount == 2:
        one = jax.random.randint(key, (), max(1, total - bound), min(bound, total - 1) + 1)
        return jnp.stack([one, total - one])
    sizes = jnp.asarray(profile(amount, total, bound, lean), jnp.int32)
    pairs = (amount - 1) // 2
    giver, receiver = sizes[1:1 + 2 * pairs:2], sizes[2:2 + 2 * pairs:2]
    room = jnp.minimum(giver - 1, bound - receiver)
    moved = jax.random.randint(jax.random.fold_in(key, 1), (pairs,), 0, 1 << 20) % (room + 1)
    sizes = sizes.at[1:1 + 2 * pairs:2].set(giver - moved).at[2:2 + 2 * pairs:2].set(receiver + moved)
    return sizes[jax.random.permutation(jax.random.fold_in(key, 2), amount)]


def setup_inputs(seed: int = 0) -> dict:
    keys = jax.random.split(jax.random.key(seed), 5)
    token_rows = draw_token_rows(jax.random.fold_in(keys[4], 71), 0)
    extra_len = jax.vmap(lambda own: ragged_sizes(own, PASS_G, ROWS_G - 15 * PASS_G, LONGEST - 15, 2))(jax.random.split(keys[1], GROUPS)).reshape((GROUPS, PASS_G)).astype(jnp.int32)
    queries = draw_queries(jax.random.fold_in(keys[4], 71), 0)
    positive = set_ends(jax.random.randint(keys[3], (QUERIES,), 0, PASSAGES), jax.random.fold_in(keys[3], 1), 0, PASSAGES - 1).astype(jnp.int32)
    return {"token_rows": token_rows, "extra_len": extra_len, "queries": queries, "positive": positive}


loss_scale = 1048576.0
inv_temp = 20.0

def group_members(extra_rows):
    lengths = (extra_rows + 15).astype(jnp.int32)
    end_rows = jnp.cumsum(lengths).astype(jnp.int32)
    first_rows = end_rows - lengths
    row_pos = jnp.arange(ROWS_G, dtype=jnp.int32)
    inside = (row_pos[None, :] >= first_rows[:, None]) & (row_pos[None, :] < end_rows[:, None])
    return (inside.astype(jnp.bfloat16), lengths)

def reference(token_rows, extra_len, queries, positive):
    group_rows = token_rows.reshape(GROUPS, ROWS_G, D)

    def pool(inputs):
        rows, extra_rows = inputs
        member, lengths = group_members(extra_rows)
        return jnp.dot(member, rows, preferred_element_type=jnp.float32) / lengths.astype(jnp.float32)[:, None]
    pooled = lax.map(pool, (group_rows, extra_len)).reshape(PASSAGES, D)
    inv_norm = lax.rsqrt(lax.optimization_barrier(jnp.sum(pooled * pooled, axis=-1, keepdims=True)) + 1e-06)
    embedding = pooled * inv_norm
    embed_half = embedding.astype(jnp.bfloat16)
    query_float = queries.astype(jnp.float32)
    query_norm = (query_float * lax.rsqrt(lax.optimization_barrier(jnp.sum(query_float * query_float, axis=-1, keepdims=True)) + 1e-06)).astype(jnp.bfloat16)
    scores = jnp.dot(query_norm, embed_half.T, preferred_element_type=jnp.float32) * inv_temp
    exp_scores = jnp.exp(scores)
    probabilities = exp_scores / lax.optimization_barrier(jnp.sum(exp_scores, axis=-1, keepdims=True))
    target = (positive[:, None] == jnp.arange(PASSAGES, dtype=jnp.int32)[None, :]).astype(jnp.float32)
    factor = loss_scale * inv_temp / QUERIES
    coefficients = ((probabilities - target) * factor).astype(jnp.bfloat16)
    d_embed = jnp.dot(coefficients.T, query_norm, preferred_element_type=jnp.float32)
    d_pooled = inv_norm * (d_embed - embedding * lax.optimization_barrier(jnp.sum(embedding * d_embed, axis=-1, keepdims=True)))
    all_lengths = (extra_len + 15).reshape(PASSAGES).astype(jnp.float32)
    d_sum = (d_pooled / all_lengths[:, None]).astype(jnp.bfloat16)

    def spread(inputs):
        extra_rows, group_grads = inputs
        member, lengths = group_members(extra_rows)
        return jnp.dot(member.T, group_grads, preferred_element_type=jnp.float32).astype(jnp.bfloat16)
    grads = lax.map(spread, (extra_len, d_sum.reshape(GROUPS, PASS_G, D)))
    return grads.reshape(TOKENS, D)
```

```python
import jax
import jax.numpy as jnp
from jax import lax
from jax.sharding import PartitionSpec as P

loss_scale = 1048576.0
inv_temp = 20.0
Z, Y, S = 16, 4, 8
Y_GROUPS = [[z * Y + y for y in range(Y)] for z in range(Z)]
Z_GROUPS = [[z * Y + y for z in range(Z)] for y in range(Y)]


def share(block, axis, count, groups=None):
    copies = jnp.broadcast_to(block[None], (count,) + block.shape)
    return lax.all_to_all(copies, axis, 0, 0, axis_index_groups=groups)


def per_device(token_rows, extra_len, queries, positive):
    row_count, width = token_rows.shape
    pass_count = extra_len.shape[1]
    seq_index = lax.axis_index("seq")
    dp_index = lax.axis_index("dp")

    query_float = queries.astype(jnp.float32)
    query_norm = (
        query_float * lax.rsqrt(jnp.sum(query_float * query_float, axis=-1, keepdims=True) + 1e-06)
    ).astype(jnp.bfloat16)
    own = queries.shape[0]
    along_z = share(query_norm, "dp", Z, Z_GROUPS).reshape(Z * own, width)
    some_queries = share(along_z, "dp", Y, Y_GROUPS).reshape(Y * Z * own, width)
    some_positive = lax.dynamic_index_in_dim(
        positive.reshape(Z, Y, S, own), seq_index, 2, keepdims=False
    )
    some_positive = some_positive.transpose(1, 0, 2).reshape(-1)

    lengths = extra_len[0] + 15
    upto = jnp.tril(jnp.ones((pass_count, pass_count), jnp.int32))
    end_rows = jnp.sum(upto * lengths[None, :], axis=1)
    first_rows = end_rows - lengths
    row_pos = seq_index * row_count + jnp.arange(row_count, dtype=jnp.int32)
    member = (
        (row_pos[None, :] >= first_rows[:, None]) & (row_pos[None, :] < end_rows[:, None])
    ).astype(jnp.bfloat16)
    partial = jnp.dot(member, token_rows, preferred_element_type=jnp.float32).astype(jnp.bfloat16)
    sums = jnp.sum(share(partial, "seq", S).astype(jnp.float32), axis=0)
    float_len = lengths.astype(jnp.float32)[:, None]
    pooled = sums / float_len
    inv_norm = lax.rsqrt(jnp.sum(pooled * pooled, axis=-1, keepdims=True) + 1e-06)
    embedding = pooled * inv_norm
    embed_half = embedding.astype(jnp.bfloat16)

    scores = (
        lax.dot_general(
            embed_half, some_queries, (((1,), (1,)), ((), ())), preferred_element_type=jnp.float32
        )
        * inv_temp
    )
    exp_scores = jnp.exp(scores)
    part_totals = jnp.sum(exp_scores, axis=0, keepdims=True)
    part_totals = jnp.sum(share(part_totals, "dp", Y, Y_GROUPS), axis=0)
    totals = jnp.sum(share(part_totals, "dp", Z, Z_GROUPS), axis=0)
    pass_ids = dp_index * pass_count + jnp.arange(pass_count, dtype=jnp.int32)
    target = (pass_ids[:, None] == some_positive[None, :]).astype(jnp.float32)
    factor = loss_scale * inv_temp / positive.shape[0]
    coefficients = ((exp_scores / totals - target) * factor).astype(jnp.bfloat16)

    d_partial = jnp.dot(coefficients, some_queries, preferred_element_type=jnp.float32)
    d_embed = jnp.sum(share(d_partial.astype(jnp.bfloat16), "seq", S).astype(jnp.float32), axis=0)
    d_pooled = inv_norm * (
        d_embed - embedding * jnp.sum(embedding * d_embed, axis=-1, keepdims=True)
    )
    d_sum = (d_pooled / float_len).astype(jnp.bfloat16)
    grads = lax.dot_general(
        member, d_sum, (((0,), (0,)), ((), ())), preferred_element_type=jnp.float32
    )
    return grads.astype(jnp.bfloat16)


def solution(mesh):
    return jax.shard_map(
        per_device,
        mesh=mesh,
        in_specs=(P(("dp", "seq"), None), P("dp", None), P(("dp", "seq"), None), P()),
        out_specs=P(("dp", "seq"), None),
        check_vma=False,
    )
```

```python
import jax
import jax.numpy as jnp
from jax import lax
from jax.sharding import PartitionSpec as P

loss_scale = 1048576.0
inv_temp = 20.0
Z, Y, S = 16, 4, 8
Z_GROUPS = [[z * Y + y for z in range(Z)] for y in range(Y)]
PLANES = [[z * Y * S + i for i in range(Y * S)] for z in range(Z)]


def share(block, axis, count, groups=None):
    copies = jnp.broadcast_to(block[None], (count,) + block.shape)
    return lax.all_to_all(copies, axis, 0, 0, axis_index_groups=groups)


def swap_seq(block, mask):
    return lax.ppermute(block, "seq", [(i, i ^ mask) for i in range(S)])


def swap_y(block, mask):
    return lax.ppermute(block, "dp", [(i, i ^ mask) for i in range(Z * Y)])


def per_device(token_rows, extra_len, queries, positive):
    row_count, width = token_rows.shape
    pass_count = extra_len.shape[1]
    own = queries.shape[0]
    seq_index = lax.axis_index("seq")
    dp_index = lax.axis_index("dp")
    z_index, y_index = dp_index // Y, dp_index % Y

    query_float = queries.astype(jnp.float32)
    query_norm = (
        query_float * lax.rsqrt(jnp.sum(query_float * query_float, axis=-1, keepdims=True) + 1e-06)
    ).astype(jnp.bfloat16)
    some_queries = share(query_norm, "dp", Z, Z_GROUPS).reshape(Z * own, width)
    some_positive = lax.dynamic_slice(
        positive.reshape(Z, Y, S, own), (0, y_index, seq_index, 0), (Z, 1, 1, own)
    ).reshape(-1)

    lengths = extra_len[0] + 15
    upto = jnp.tril(jnp.ones((pass_count, pass_count), jnp.int32))
    end_rows = jnp.sum(upto * lengths[None, :], axis=1)
    first_rows = end_rows - lengths
    row_pos = seq_index * row_count + jnp.arange(row_count, dtype=jnp.int32)
    member = (
        (row_pos[None, :] >= first_rows[:, None]) & (row_pos[None, :] < end_rows[:, None])
    ).astype(jnp.bfloat16)
    sums = jnp.dot(member, token_rows, preferred_element_type=jnp.float32)
    for mask in (1, 2, 6):
        sums = sums + swap_seq(sums.astype(jnp.bfloat16), mask).astype(jnp.float32)
    float_len = lengths.astype(jnp.float32)[:, None]
    pooled = sums / float_len
    inv_norm = lax.rsqrt(jnp.sum(pooled * pooled, axis=-1, keepdims=True) + 1e-06)
    embedding = pooled * inv_norm

    near = embedding.astype(jnp.bfloat16)[None]
    near = jnp.concatenate([near, swap_y(near, 1)], axis=0)
    far = swap_y(near, 3)

    def score(blocks):
        return lax.dot_general(
            blocks, some_queries, (((2,), (1,)), ((), ())), preferred_element_type=jnp.float32
        )

    near_scores, far_scores = score(near), score(far)
    by_mask = [near_scores[0], near_scores[1], far_scores[1], far_scores[0]]
    ordered = []
    for y in range(Y):
        mask = y_index ^ y
        picked = by_mask[0]
        for other in range(1, Y):
            picked = jnp.where(mask == other, by_mask[other], picked)
        ordered.append(picked)
    scores = jnp.concatenate(ordered, axis=0) * inv_temp
    exp_scores = jnp.exp(scores)
    part_totals = jnp.sum(exp_scores, axis=0, keepdims=True)
    totals = jnp.sum(share(part_totals, "dp", Z, Z_GROUPS), axis=0)
    pass_ids = z_index * Y * pass_count + jnp.arange(Y * pass_count, dtype=jnp.int32)
    target = (pass_ids[:, None] == some_positive[None, :]).astype(jnp.float32)
    factor = loss_scale * inv_temp / positive.shape[0]
    coefficients = ((exp_scores / totals - target) * factor).astype(jnp.bfloat16)

    slots = pass_count // S
    d_partial = jnp.dot(coefficients, some_queries, preferred_element_type=jnp.float32)
    d_partial = d_partial.astype(jnp.bfloat16).reshape(Y * S, slots, width)
    d_parts = lax.all_to_all(d_partial, ("dp", "seq"), 0, 0, axis_index_groups=PLANES)
    d_embed = jnp.sum(d_parts.astype(jnp.float32), axis=0)
    first = seq_index * slots
    own_embedding = lax.dynamic_slice_in_dim(embedding, first, slots, 0)
    own_norm = lax.dynamic_slice_in_dim(inv_norm, first, slots, 0)
    own_len = lax.dynamic_slice_in_dim(float_len, first, slots, 0)
    d_pooled = own_norm * (
        d_embed - own_embedding * jnp.sum(own_embedding * d_embed, axis=-1, keepdims=True)
    )
    d_sum = (d_pooled / own_len).astype(jnp.bfloat16)
    every_d_sum = share(d_sum, "seq", S).reshape(pass_count, width)
    grads = lax.dot_general(
        member, every_d_sum, (((0,), (0,)), ((), ())), preferred_element_type=jnp.float32
    )
    return grads.astype(jnp.bfloat16)


def solution(mesh):
    return jax.shard_map(
        per_device,
        mesh=mesh,
        in_specs=(P(("dp", "seq"), None), P("dp", None), P(("dp", "seq"), None), P()),
        out_specs=P(("dp", "seq"), None),
        check_vma=False,
    )
```

```python
import jax
import jax.numpy as jnp
from jax import lax
from jax.sharding import PartitionSpec as P

loss_scale = 1048576.0
inv_temp = 20.0
DP, S = 64, 8


def share(block, axis, count):
    copies = jnp.broadcast_to(block[None], (count,) + block.shape)
    return lax.all_to_all(copies, axis, 0, 0)


def swap_seq(block, mask):
    return lax.ppermute(block, "seq", [(i, i ^ mask) for i in range(S)])


def per_device(token_rows, extra_len, queries, positive):
    row_count, width = token_rows.shape
    pass_count = extra_len.shape[1]
    own = queries.shape[0]
    seq_index = lax.axis_index("seq")
    dp_index = lax.axis_index("dp")

    raw = share(queries, "dp", DP).reshape(DP * own, width).astype(jnp.float32)
    some_queries = (
        raw * lax.rsqrt(jnp.sum(raw * raw, axis=-1, keepdims=True) + 1e-06)
    ).astype(jnp.bfloat16)
    some_positive = lax.dynamic_index_in_dim(
        positive.reshape(DP, S, own), seq_index, 1, keepdims=False
    ).reshape(-1)

    lengths = extra_len[0] + 15
    upto = jnp.tril(jnp.ones((pass_count, pass_count), jnp.int32))
    end_rows = jnp.sum(upto * lengths[None, :], axis=1)
    first_rows = end_rows - lengths
    row_pos = seq_index * row_count + jnp.arange(row_count, dtype=jnp.int32)
    member = (
        (row_pos[None, :] >= first_rows[:, None]) & (row_pos[None, :] < end_rows[:, None])
    ).astype(jnp.bfloat16)
    sums = jnp.dot(member, token_rows, preferred_element_type=jnp.float32)
    for mask in (1, 2, 6):
        sums = sums + swap_seq(sums.astype(jnp.bfloat16), mask).astype(jnp.float32)
    float_len = lengths.astype(jnp.float32)[:, None]
    pooled = sums / float_len
    inv_norm = lax.rsqrt(jnp.sum(pooled * pooled, axis=-1, keepdims=True) + 1e-06)
    embedding = pooled * inv_norm
    embed_half = embedding.astype(jnp.bfloat16)

    scores = (
        lax.dot_general(
            embed_half, some_queries, (((1,), (1,)), ((), ())), preferred_element_type=jnp.float32
        )
        * inv_temp
    )
    exp_scores = jnp.exp(scores)
    part_totals = jnp.sum(exp_scores, axis=0, keepdims=True)
    totals = jnp.sum(share(part_totals, "dp", DP), axis=0)
    pass_ids = dp_index * pass_count + jnp.arange(pass_count, dtype=jnp.int32)
    target = (pass_ids[:, None] == some_positive[None, :]).astype(jnp.float32)
    factor = loss_scale * inv_temp / positive.shape[0]
    coefficients = ((exp_scores / totals - target) * factor).astype(jnp.bfloat16)

    slots = pass_count // S
    d_partial = jnp.dot(coefficients, some_queries, preferred_element_type=jnp.float32)
    d_partial = d_partial.astype(jnp.bfloat16).reshape(S, slots, width)
    d_parts = lax.all_to_all(d_partial, "seq", 0, 0)
    d_embed = jnp.sum(d_parts.astype(jnp.float32), axis=0)
    first = seq_index * slots
    own_embedding = lax.dynamic_slice_in_dim(embedding, first, slots, 0)
    own_norm = lax.dynamic_slice_in_dim(inv_norm, first, slots, 0)
    own_len = lax.dynamic_slice_in_dim(float_len, first, slots, 0)
    d_pooled = own_norm * (
        d_embed - own_embedding * jnp.sum(own_embedding * d_embed, axis=-1, keepdims=True)
    )
    d_sum = (d_pooled / own_len).astype(jnp.bfloat16)
    every_d_sum = share(d_sum, "seq", S).reshape(pass_count, width)
    grads = lax.dot_general(
        member, every_d_sum, (((0,), (0,)), ((), ())), preferred_element_type=jnp.float32
    )
    return grads.astype(jnp.bfloat16)


def solution(mesh):
    return jax.shard_map(
        per_device,
        mesh=mesh,
        in_specs=(P(("dp", "seq"), None), P("dp", None), P(("dp", "seq"), None), P()),
        out_specs=P(("dp", "seq"), None),
        check_vma=False,
    )
```

```python
import jax
import jax.numpy as jnp
from jax import lax
from jax.sharding import PartitionSpec as P

loss_scale = 1048576.0
inv_temp = 20.0
Z, Y, S = 16, 4, 8
Z_GROUPS = [[z * Y + y for z in range(Z)] for y in range(Y)]
PAIRS = [[p * 2 * S + i for i in range(2 * S)] for p in range(Z * Y // 2)]
LINES = [[z * Y + y for z in range(Z) for y in (low, 3 - low)] for low in range(2)]


def share(block, axis, count, groups=None):
    copies = jnp.broadcast_to(block[None], (count,) + block.shape)
    return lax.all_to_all(copies, axis, 0, 0, axis_index_groups=groups)


def swap_seq(block, mask):
    return lax.ppermute(block, "seq", [(i, i ^ mask) for i in range(S)])


def swap_y(block, mask):
    return lax.ppermute(block, "dp", [(i, i ^ mask) for i in range(Z * Y)])


def per_device(token_rows, extra_len, queries, positive):
    row_count, width = token_rows.shape
    pass_count = extra_len.shape[1]
    own = queries.shape[0]
    seq_index = lax.axis_index("seq")
    dp_index = lax.axis_index("dp")
    y_index = dp_index & (Y - 1)

    query_float = queries.astype(jnp.float32)
    query_norm = (
        query_float * lax.rsqrt(jnp.sum(query_float * query_float, axis=-1, keepdims=True) + 1e-06)
    ).astype(jnp.bfloat16)
    own_line = share(query_norm, "dp", Z, Z_GROUPS).reshape(Z * own, width)
    other_line = swap_y(own_line, 3)
    by_line = positive.reshape(Z, Y, S, own)

    def line_positive(y):
        return lax.dynamic_slice(by_line, (0, y, seq_index, 0), (Z, 1, 1, own)).reshape(-1)

    lengths = extra_len[0] + 15
    upto = jnp.tril(jnp.ones((pass_count, pass_count), jnp.int32))
    end_rows = jnp.sum(upto * lengths[None, :], axis=1)
    first_rows = end_rows - lengths
    row_pos = seq_index * row_count + jnp.arange(row_count, dtype=jnp.int32)
    member = (
        (row_pos[None, :] >= first_rows[:, None]) & (row_pos[None, :] < end_rows[:, None])
    ).astype(jnp.bfloat16)
    sums = jnp.dot(member, token_rows, preferred_element_type=jnp.float32)
    for mask in (1, 2, 6):
        sums = sums + swap_seq(sums.astype(jnp.bfloat16), mask).astype(jnp.float32)
    float_len = lengths.astype(jnp.float32)[:, None]
    pooled = sums / float_len
    inv_norm = lax.rsqrt(jnp.sum(pooled * pooled, axis=-1, keepdims=True) + 1e-06)
    embedding = pooled * inv_norm

    odd = (y_index & 1) == 1
    embed_half = embedding.astype(jnp.bfloat16)
    beside = swap_y(embed_half, 1)
    embeds = jnp.concatenate(
        [jnp.where(odd, beside, embed_half), jnp.where(odd, embed_half, beside)], axis=0
    )

    def exp_scores(line):
        return jnp.exp(
            lax.dot_general(
                embeds, line, (((1,), (1,)), ((), ())), preferred_element_type=jnp.float32
            )
            * inv_temp
        )

    own_exp, other_exp = exp_scores(own_line), exp_scores(other_line)
    own_part, other_part = jnp.sum(own_exp, axis=0), jnp.sum(other_exp, axis=0)
    high = y_index >= 2
    parts = jnp.stack([jnp.where(high, other_part, own_part), jnp.where(high, own_part, other_part)])
    totals = jnp.sum(share(parts, "dp", 2 * Z, LINES), axis=0)
    own_total = jnp.where(high, totals[1], totals[0])
    other_total = jnp.where(high, totals[0], totals[1])
    pass_ids = (dp_index - (y_index & 1)) * pass_count + jnp.arange(2 * pass_count, dtype=jnp.int32)
    factor = loss_scale * inv_temp / positive.shape[0]

    def coefficients(exps, total, y):
        target = (pass_ids[:, None] == line_positive(y)[None, :]).astype(jnp.float32)
        return ((exps / total[None, :] - target) * factor).astype(jnp.bfloat16)

    slots = pass_count // S
    d_partial = jnp.dot(
        coefficients(own_exp, own_total, y_index), own_line, preferred_element_type=jnp.float32
    ) + jnp.dot(
        coefficients(other_exp, other_total, 3 - y_index),
        other_line,
        preferred_element_type=jnp.float32,
    )
    d_partial = d_partial.astype(jnp.bfloat16).reshape(2 * S, slots, width)
    d_parts = lax.all_to_all(d_partial, ("dp", "seq"), 0, 0, axis_index_groups=PAIRS)
    d_embed = jnp.sum(d_parts.astype(jnp.float32), axis=0)
    first = seq_index * slots
    own_embedding = lax.dynamic_slice_in_dim(embedding, first, slots, 0)
    own_norm = lax.dynamic_slice_in_dim(inv_norm, first, slots, 0)
    own_len = lax.dynamic_slice_in_dim(float_len, first, slots, 0)
    d_pooled = own_norm * (
        d_embed - own_embedding * jnp.sum(own_embedding * d_embed, axis=-1, keepdims=True)
    )
    d_sum = (d_pooled / own_len).astype(jnp.bfloat16)
    every_d_sum = share(d_sum, "seq", S).reshape(pass_count, width)
    grads = lax.dot_general(
        member, every_d_sum, (((0,), (0,)), ((), ())), preferred_element_type=jnp.float32
    )
    return grads.astype(jnp.bfloat16)


def solution(mesh):
    return jax.shard_map(
        per_device,
        mesh=mesh,
        in_specs=(P(("dp", "seq"), None), P("dp", None), P(("dp", "seq"), None), P()),
        out_specs=P(("dp", "seq"), None),
        check_vma=False,
    )
```

```python
import jax
import jax.numpy as jnp
from jax import lax
from jax.sharding import PartitionSpec as P

loss_scale = 1048576.0
inv_temp = 20.0
Z, Y, S = 16, 4, 8
Z_GROUPS = [[z * Y + y for z in range(Z)] for y in range(Y)]
PAIRS = [[p * 2 * S + i for i in range(2 * S)] for p in range(Z * Y // 2)]
LINES = [
    [(z + Z // 2) % Z * Y + y for z in range(Z) for y in (low, 3 - low)] for low in range(2)
]


def share(block, axis, count, groups=None):
    copies = jnp.broadcast_to(block[None], (count,) + block.shape)
    return lax.all_to_all(copies, axis, 0, 0, axis_index_groups=groups)


def swap_seq(block, mask):
    return lax.ppermute(block, "seq", [(i, i ^ mask) for i in range(S)])


def swap_y(block, mask):
    return lax.ppermute(block, "dp", [(i, i ^ mask) for i in range(Z * Y)])


def per_device(token_rows, extra_len, queries, positive):
    row_count, width = token_rows.shape
    pass_count = extra_len.shape[1]
    own = queries.shape[0]
    seq_index = lax.axis_index("seq")
    dp_index = lax.axis_index("dp")
    y_index = dp_index & (Y - 1)

    query_float = queries.astype(jnp.float32)
    query_norm = (
        query_float * lax.rsqrt(jnp.sum(query_float * query_float, axis=-1, keepdims=True) + 1e-06)
    ).astype(jnp.bfloat16)
    own_line = share(query_norm, "dp", Z, Z_GROUPS).reshape(Z * own, width)
    other_line = swap_y(own_line, 3)
    by_line = positive.reshape(Z, Y, S, own)

    def line_positive(y):
        return lax.dynamic_slice(by_line, (0, y, seq_index, 0), (Z, 1, 1, own)).reshape(-1)

    lengths = extra_len[0] + 15
    upto = jnp.tril(jnp.ones((pass_count, pass_count), jnp.int32))
    end_rows = jnp.sum(upto * lengths[None, :], axis=1)
    first_rows = end_rows - lengths
    row_pos = seq_index * row_count + jnp.arange(row_count, dtype=jnp.int32)
    member = (
        (row_pos[None, :] >= first_rows[:, None]) & (row_pos[None, :] < end_rows[:, None])
    ).astype(jnp.bfloat16)
    sums = jnp.dot(member, token_rows, preferred_element_type=jnp.float32)

    def over_seq(step, sums):
        for mask in (1, 2, 6):
            sums = sums + swap_seq(sums.astype(jnp.bfloat16), mask).astype(jnp.float32)
        return sums

    sums = lax.fori_loop(0, jnp.minimum(lengths[0], 1), over_seq, sums)
    float_len = lengths.astype(jnp.float32)[:, None]
    pooled = sums / float_len
    inv_norm = lax.rsqrt(jnp.sum(pooled * pooled, axis=-1, keepdims=True) + 1e-06)
    embedding = pooled * inv_norm

    odd = (y_index & 1) == 1
    embed_half = embedding.astype(jnp.bfloat16)
    beside = swap_y(embed_half, 1)
    embeds = jnp.concatenate(
        [jnp.where(odd, beside, embed_half), jnp.where(odd, embed_half, beside)], axis=0
    )

    def exp_scores(line):
        return jnp.exp(
            lax.dot_general(
                embeds, line, (((1,), (1,)), ((), ())), preferred_element_type=jnp.float32
            )
            * inv_temp
        )

    own_exp, other_exp = exp_scores(own_line), exp_scores(other_line)
    own_part, other_part = jnp.sum(own_exp, axis=0), jnp.sum(other_exp, axis=0)
    high = y_index >= 2
    parts = jnp.stack([jnp.where(high, other_part, own_part), jnp.where(high, own_part, other_part)])
    totals = jnp.sum(share(parts, "dp", 2 * Z, LINES), axis=0)
    own_total = jnp.where(high, totals[1], totals[0])
    other_total = jnp.where(high, totals[0], totals[1])
    pass_ids = (dp_index - (y_index & 1)) * pass_count + jnp.arange(2 * pass_count, dtype=jnp.int32)
    factor = loss_scale * inv_temp / positive.shape[0]

    def coefficients(exps, total, y):
        target = (pass_ids[:, None] == line_positive(y)[None, :]).astype(jnp.float32)
        return ((exps / total[None, :] - target) * factor).astype(jnp.bfloat16)

    slots = pass_count // S
    d_partial = jnp.dot(
        coefficients(own_exp, own_total, y_index), own_line, preferred_element_type=jnp.float32
    ) + jnp.dot(
        coefficients(other_exp, other_total, 3 - y_index),
        other_line,
        preferred_element_type=jnp.float32,
    )
    d_partial = d_partial.astype(jnp.bfloat16).reshape(2 * S, slots, width)
    d_parts = lax.all_to_all(d_partial, ("dp", "seq"), 0, 0, axis_index_groups=PAIRS)
    d_embed = jnp.sum(d_parts.astype(jnp.float32), axis=0)
    first = seq_index * slots
    own_embedding = lax.dynamic_slice_in_dim(embedding, first, slots, 0)
    own_norm = lax.dynamic_slice_in_dim(inv_norm, first, slots, 0)
    own_len = lax.dynamic_slice_in_dim(float_len, first, slots, 0)
    d_pooled = own_norm * (
        d_embed - own_embedding * jnp.sum(own_embedding * d_embed, axis=-1, keepdims=True)
    )
    d_sum = (d_pooled / own_len).astype(jnp.bfloat16)
    every_d_sum = share(d_sum, "seq", S).reshape(pass_count, width)
    grads = lax.dot_general(
        member, every_d_sum, (((0,), (0,)), ((), ())), preferred_element_type=jnp.float32
    )
    return grads.astype(jnp.bfloat16)


def solution(mesh):
    return jax.shard_map(
        per_device,
        mesh=mesh,
        in_specs=(P(("dp", "seq"), None), P("dp", None), P(("dp", "seq"), None), P()),
        out_specs=P(("dp", "seq"), None),
        check_vma=False,
    )
```

```python
import jax
import jax.numpy as jnp
from jax import lax
from jax.experimental import pallas as pl
from jax.experimental.pallas import tpu as pltpu
from jax.sharding import PartitionSpec as P

loss_scale = 1048576.0
inv_temp = 20.0
Z, Y, S = 16, 4, 8
Z_GROUPS = [[z * Y + y for z in range(Z)] for y in range(Y)]
PAIRS = [[p * 2 * S + i for i in range(2 * S)] for p in range(Z * Y // 2)]
LINES = [
    [(z + Z // 2) % Z * Y + y for z in range(Z) for y in (low, 3 - low)] for low in range(2)
]


def share(block, axis, count, groups=None):
    copies = jnp.broadcast_to(block[None], (count,) + block.shape)
    return lax.all_to_all(copies, axis, 0, 0, axis_index_groups=groups)


def normalized_copies(queries, count):
    def kernel(in_ref, out_ref):
        query = in_ref[...].astype(jnp.float32)
        scale = lax.rsqrt(jnp.sum(query * query, axis=-1, keepdims=True) + 1e-06)
        rounded = (query * scale).astype(jnp.bfloat16)
        for i in range(count):
            out_ref[i] = rounded

    return pl.pallas_call(
        kernel,
        out_shape=jax.ShapeDtypeStruct((count,) + queries.shape, jnp.bfloat16),
        in_specs=[pl.BlockSpec(memory_space=pltpu.VMEM)],
        out_specs=pl.BlockSpec(memory_space=pltpu.VMEM),
        compiler_params=pltpu.CompilerParams(vmem_limit_bytes=8 << 20),
        name="normalized_copies",
    )(queries)


def swap_seq(block, mask):
    return lax.ppermute(block, "seq", [(i, i ^ mask) for i in range(S)])


def swap_y(block, mask):
    return lax.ppermute(block, "dp", [(i, i ^ mask) for i in range(Z * Y)])


def per_device(token_rows, extra_len, queries, positive):
    row_count, width = token_rows.shape
    pass_count = extra_len.shape[1]
    own = queries.shape[0]
    seq_index = lax.axis_index("seq")
    dp_index = lax.axis_index("dp")
    y_index = dp_index & (Y - 1)

    copies = normalized_copies(queries, Z)
    own_line = lax.all_to_all(copies, "dp", 0, 0, axis_index_groups=Z_GROUPS)
    own_line = own_line.reshape(Z * own, width)
    by_line = positive.reshape(Z, Y, S, own)

    def line_positive(y):
        return lax.dynamic_slice(by_line, (0, y, seq_index, 0), (Z, 1, 1, own)).reshape(-1)

    lengths = lax.optimization_barrier(extra_len[0] + 15)
    upto = jnp.tril(jnp.ones((pass_count, pass_count), jnp.int32))
    end_rows = jnp.sum(upto * lengths[None, :], axis=1)
    first_rows = end_rows - lengths
    row_pos = seq_index * row_count + jnp.arange(row_count, dtype=jnp.int32)
    member = (
        (row_pos[None, :] >= first_rows[:, None]) & (row_pos[None, :] < end_rows[:, None])
    ).astype(jnp.bfloat16)
    sums = jnp.dot(member, token_rows, preferred_element_type=jnp.float32)

    def over_seq(step, sums):
        for mask in (1, 2, 6):
            sums = sums + swap_seq(sums.astype(jnp.bfloat16), mask).astype(jnp.float32)
        return sums

    sums = lax.fori_loop(0, jnp.minimum(lengths[0], 1), over_seq, sums)
    float_len = lengths.astype(jnp.float32)[:, None]
    pooled = sums / float_len
    inv_norm = lax.rsqrt(jnp.sum(pooled * pooled, axis=-1, keepdims=True) + 1e-06)
    embedding = pooled * inv_norm

    odd = (y_index & 1) == 1
    embed_half, own_line = lax.optimization_barrier((embedding.astype(jnp.bfloat16), own_line))
    own_line, other_line, beside = lax.optimization_barrier(
        (own_line, swap_y(own_line, 3), swap_y(embed_half, 1))
    )
    embeds = jnp.concatenate(
        [jnp.where(odd, beside, embed_half), jnp.where(odd, embed_half, beside)], axis=0
    )

    def exp_scores(line):
        return jnp.exp(
            lax.dot_general(
                embeds, line, (((1,), (1,)), ((), ())), preferred_element_type=jnp.float32
            )
            * inv_temp
        )

    own_exp, other_exp = exp_scores(own_line), exp_scores(other_line)
    own_part, other_part = jnp.sum(own_exp, axis=0), jnp.sum(other_exp, axis=0)
    high = y_index >= 2
    parts = jnp.stack([jnp.where(high, other_part, own_part), jnp.where(high, own_part, other_part)])
    totals = jnp.sum(share(parts, "dp", 2 * Z, LINES), axis=0)
    own_total = jnp.where(high, totals[1], totals[0])
    other_total = jnp.where(high, totals[0], totals[1])
    pass_ids = (dp_index - (y_index & 1)) * pass_count + jnp.arange(2 * pass_count, dtype=jnp.int32)
    factor = loss_scale * inv_temp / positive.shape[0]

    def coefficients(exps, total, y):
        target = (pass_ids[:, None] == line_positive(y)[None, :]).astype(jnp.float32)
        return ((exps / total[None, :] - target) * factor).astype(jnp.bfloat16)

    slots = pass_count // S
    d_partial = jnp.dot(
        coefficients(own_exp, own_total, y_index), own_line, preferred_element_type=jnp.float32
    ) + jnp.dot(
        coefficients(other_exp, other_total, 3 - y_index),
        other_line,
        preferred_element_type=jnp.float32,
    )
    d_partial = d_partial.astype(jnp.bfloat16).reshape(2 * S, slots, width)
    d_parts = lax.all_to_all(d_partial, ("dp", "seq"), 0, 0, axis_index_groups=PAIRS)
    d_embed = jnp.sum(d_parts.astype(jnp.float32), axis=0)
    first = seq_index * slots
    own_embedding = lax.dynamic_slice_in_dim(embedding, first, slots, 0)
    own_norm = lax.dynamic_slice_in_dim(inv_norm, first, slots, 0)
    own_len = lax.dynamic_slice_in_dim(float_len, first, slots, 0)
    d_pooled = own_norm * (
        d_embed - own_embedding * jnp.sum(own_embedding * d_embed, axis=-1, keepdims=True)
    )
    d_sum = (d_pooled / own_len).astype(jnp.bfloat16)
    every_d_sum = share(d_sum, "seq", S).reshape(pass_count, width)
    grads = lax.dot_general(
        member, every_d_sum, (((0,), (0,)), ((), ())), preferred_element_type=jnp.float32
    )
    return grads.astype(jnp.bfloat16)


def solution(mesh):
    return jax.shard_map(
        per_device,
        mesh=mesh,
        in_specs=(P(("dp", "seq"), None), P("dp", None), P(("dp", "seq"), None), P()),
        out_specs=P(("dp", "seq"), None),
        check_vma=False,
    )
```

```python
import jax
import jax.numpy as jnp
from jax import lax
from jax.experimental import pallas as pl
from jax.experimental.pallas import tpu as pltpu
from jax.sharding import PartitionSpec as P

loss_scale = 1048576.0
inv_temp = 20.0
Z, Y, S = 16, 4, 8
Z_GROUPS = [[z * Y + y for z in range(Z)] for y in range(Y)]
PAIRS = [[p * 2 * S + i for i in range(2 * S)] for p in range(Z * Y // 2)]
LINES = [
    [(z + Z // 2) % Z * Y + y for z in range(Z) for y in (low, 3 - low)] for low in range(2)
]


def share(block, axis, count, groups=None):
    copies = jnp.broadcast_to(block[None], (count,) + block.shape)
    return lax.all_to_all(copies, axis, 0, 0, axis_index_groups=groups)


def normalized_copies(queries, count):
    def kernel(in_ref, out_ref):
        query = in_ref[...].astype(jnp.float32)
        scale = lax.rsqrt(jnp.sum(query * query, axis=-1, keepdims=True) + 1e-06)
        rounded = (query * scale).astype(jnp.bfloat16)
        for i in range(count):
            out_ref[i] = rounded

    return pl.pallas_call(
        kernel,
        out_shape=jax.ShapeDtypeStruct((count,) + queries.shape, jnp.bfloat16),
        in_specs=[pl.BlockSpec(memory_space=pltpu.VMEM)],
        out_specs=pl.BlockSpec(memory_space=pltpu.VMEM),
        compiler_params=pltpu.CompilerParams(vmem_limit_bytes=8 << 20),
        name="normalized_copies",
    )(queries)


def dot_rows(left, right):
    return lax.dot_general(
        left, right, (((1,), (1,)), ((), ())), preferred_element_type=jnp.float32
    )


def score(embeds, own_line, other_line, count):
    passes, queries = embeds[0].shape[0], own_line.shape[0]

    def kernel(here_ref, beside_ref, own_ref, other_ref, own_out, other_out, sums_out):
        y_index = lax.axis_index("dp") & (Y - 1)
        odd, high = (y_index & 1) == 1, y_index >= 2
        embeddings = jnp.concatenate([here_ref[...], beside_ref[...]], axis=0)
        parts = []
        for line_ref, out_ref in ((own_ref, own_out), (other_ref, other_out)):
            line = line_ref[...]
            quarter = line.shape[1] // 4
            dots = [
                dot_rows(
                    embeddings[:, k * quarter : (k + 1) * quarter],
                    line[:, k * quarter : (k + 1) * quarter],
                )
                for k in range(4)
            ]
            exps = jnp.exp((dots[0] + dots[1] + dots[2] + dots[3]) * inv_temp)
            out_ref[:passes] = jnp.where(odd, exps[passes:], exps[:passes])
            out_ref[passes:] = jnp.where(odd, exps[:passes], exps[passes:])
            parts.append(jnp.sum(exps, axis=0, keepdims=True))
        first = jnp.where(high, parts[1], parts[0])
        second = jnp.where(high, parts[0], parts[1])
        row = lax.broadcasted_iota(jnp.int32, (2, queries), 0)
        both = jnp.where(row == 0, first, second)
        sums_out[...] = jnp.broadcast_to(both[None], sums_out.shape)

    vmem = pl.BlockSpec(memory_space=pltpu.VMEM)
    exps = jax.ShapeDtypeStruct((2 * passes, queries), jnp.float32)
    return pl.pallas_call(
        kernel,
        out_shape=(exps, exps, jax.ShapeDtypeStruct((count, 2, queries), jnp.float32)),
        in_specs=[vmem] * 4,
        out_specs=(vmem, vmem, vmem),
        compiler_params=pltpu.CompilerParams(vmem_limit_bytes=16 << 20),
        name="score",
    )(*embeds, own_line, other_line)


def gradients(own_exp, other_exp, part_totals, own_line, other_line, own_at, other_at, factor):
    passes, queries = own_exp.shape
    width = own_line.shape[1] // S

    def kernel(
        own_exp_ref, other_exp_ref, totals_ref, own_ref, other_ref, own_at_ref, other_at_ref, out_ref
    ):
        dp_index = lax.axis_index("dp")
        high = (dp_index & (Y - 1)) >= 2
        totals = jnp.sum(totals_ref[...], axis=0)
        low_total, high_total = totals[0:1], totals[1:2]
        passage = lax.broadcasted_iota(jnp.int32, (passes, queries), 0)
        passage += (dp_index - (dp_index & 1)) * (passes // 2)

        def coefficients(exp_ref, total, at_ref):
            target = (passage == at_ref[...]).astype(jnp.float32)
            return ((exp_ref[...] / total - target) * factor).astype(jnp.bfloat16)

        own = coefficients(own_exp_ref, jnp.where(high, high_total, low_total), own_at_ref)
        other = coefficients(other_exp_ref, jnp.where(high, low_total, high_total), other_at_ref)
        for part in range(S):
            columns = pl.ds(part * width, width)
            block = jnp.dot(
                own, own_ref[:, columns], preferred_element_type=jnp.float32
            ) + jnp.dot(other, other_ref[:, columns], preferred_element_type=jnp.float32)
            block = block.astype(jnp.bfloat16)
            out_ref[part] = block[: passes // 2]
            out_ref[S + part] = block[passes // 2 :]

    vmem = pl.BlockSpec(memory_space=pltpu.VMEM)
    return pl.pallas_call(
        kernel,
        out_shape=jax.ShapeDtypeStruct((2 * S, passes // 2, width), jnp.bfloat16),
        in_specs=[vmem] * 7,
        out_specs=vmem,
        compiler_params=pltpu.CompilerParams(vmem_limit_bytes=16 << 20),
        name="gradients",
    )(own_exp, other_exp, part_totals, own_line, other_line, own_at, other_at)


def swap_seq(block, mask):
    return lax.ppermute(block, "seq", [(i, i ^ mask) for i in range(S)])


def swap_y(block, mask):
    return lax.ppermute(block, "dp", [(i, i ^ mask) for i in range(Z * Y)])


def per_device(token_rows, extra_len, queries, positive):
    row_count, width = token_rows.shape
    pass_count = extra_len.shape[1]
    own = queries.shape[0]
    seq_index = lax.axis_index("seq")
    dp_index = lax.axis_index("dp")
    y_index = dp_index & (Y - 1)

    copies = normalized_copies(queries, Z)
    own_line = lax.all_to_all(copies, "dp", 0, 0, axis_index_groups=Z_GROUPS)
    own_line = own_line.reshape(Z * own, width)
    by_line = positive.reshape(Z, Y, S, own)

    def line_positive(y):
        return lax.dynamic_slice(by_line, (0, y, seq_index, 0), (Z, 1, 1, own)).reshape(-1)

    lengths = lax.optimization_barrier(extra_len[0] + 15)
    upto = jnp.tril(jnp.ones((pass_count, pass_count), jnp.int32))
    end_rows = jnp.sum(upto * lengths[None, :], axis=1)
    first_rows = end_rows - lengths
    row_pos = seq_index * row_count + jnp.arange(row_count, dtype=jnp.int32)
    member = (
        (row_pos[None, :] >= first_rows[:, None]) & (row_pos[None, :] < end_rows[:, None])
    ).astype(jnp.bfloat16)
    sums = jnp.dot(member, token_rows, preferred_element_type=jnp.float32)

    def over_seq(step, sums):
        for mask in (1, 2, 6):
            sums = sums + swap_seq(sums.astype(jnp.bfloat16), mask).astype(jnp.float32)
        return sums

    sums = lax.fori_loop(0, jnp.minimum(lengths[0], 1), over_seq, sums)
    float_len = lengths.astype(jnp.float32)[:, None]
    pooled = sums / float_len
    inv_norm = lax.rsqrt(jnp.sum(pooled * pooled, axis=-1, keepdims=True) + 1e-06)
    embedding = pooled * inv_norm

    embed_half, own_line = lax.optimization_barrier((embedding.astype(jnp.bfloat16), own_line))
    own_line, other_line, beside = lax.optimization_barrier(
        (own_line, swap_y(own_line, 3), swap_y(embed_half, 1))
    )
    own_exp, other_exp, parts = score((embed_half, beside), own_line, other_line, 2 * Z)
    part_totals = lax.all_to_all(parts, "dp", 0, 0, axis_index_groups=LINES)

    d_partial = gradients(
        own_exp,
        other_exp,
        part_totals,
        own_line,
        other_line,
        line_positive(y_index)[None, :],
        line_positive(3 - y_index)[None, :],
        loss_scale * inv_temp / positive.shape[0],
    )
    d_parts = lax.all_to_all(d_partial, ("dp", "seq"), 0, 0, axis_index_groups=PAIRS)
    d_own = jnp.sum(d_parts.astype(jnp.float32), axis=0).astype(jnp.bfloat16)
    d_embed = share(d_own, "seq", S).transpose(1, 0, 2).reshape(pass_count, width)
    d_embed = d_embed.astype(jnp.float32)
    d_pooled = inv_norm * (
        d_embed - embedding * jnp.sum(embedding * d_embed, axis=-1, keepdims=True)
    )
    every_d_sum = (d_pooled / float_len).astype(jnp.bfloat16)
    grads = lax.dot_general(
        member, every_d_sum, (((0,), (0,)), ((), ())), preferred_element_type=jnp.float32
    )
    return grads.astype(jnp.bfloat16)


def solution(mesh):
    return jax.shard_map(
        per_device,
        mesh=mesh,
        in_specs=(P(("dp", "seq"), None), P("dp", None), P(("dp", "seq"), None), P()),
        out_specs=P(("dp", "seq"), None),
        check_vma=False,
    )
```

```python
import jax
import jax.numpy as jnp
from jax import lax
from jax.experimental import pallas as pl
from jax.experimental.pallas import tpu as pltpu
from jax.sharding import PartitionSpec as P

loss_scale = 1048576.0
inv_temp = 20.0
Z, Y, S = 16, 4, 8
FIRST, SECOND = 14, 8
Z_GROUPS = [[(z + FIRST) % Z * Y + y for z in range(Z)] for y in range(Y)]
PAIRS = [[p * 2 * S + i for i in range(2 * S)] for p in range(Z * Y // 2)]
LINES = [
    [(z + SECOND) % Z * Y + y for z in range(Z) for y in (low, 3 - low)] for low in range(2)
]


def share(block, axis, count, groups=None):
    copies = jnp.broadcast_to(block[None], (count,) + block.shape)
    return lax.all_to_all(copies, axis, 0, 0, axis_index_groups=groups)


def normalized_copies(queries, count):
    def kernel(in_ref, out_ref):
        query = in_ref[...].astype(jnp.float32)
        scale = lax.rsqrt(jnp.sum(query * query, axis=-1, keepdims=True) + 1e-06)
        rounded = (query * scale).astype(jnp.bfloat16)
        for i in range(count):
            out_ref[i] = rounded

    return pl.pallas_call(
        kernel,
        out_shape=jax.ShapeDtypeStruct((count,) + queries.shape, jnp.bfloat16),
        in_specs=[pl.BlockSpec(memory_space=pltpu.VMEM)],
        out_specs=pl.BlockSpec(memory_space=pltpu.VMEM),
        compiler_params=pltpu.CompilerParams(vmem_limit_bytes=8 << 20),
        name="normalized_copies",
    )(queries)


def dot_rows(left, right):
    return lax.dot_general(
        left, right, (((1,), (1,)), ((), ())), preferred_element_type=jnp.float32
    )


def score(embeds, own_line, other_line, count):
    passes, queries = embeds[0].shape[0], own_line.shape[0]

    def kernel(here_ref, beside_ref, own_ref, other_ref, own_out, other_out, sums_out):
        y_index = lax.axis_index("dp") & (Y - 1)
        odd, high = (y_index & 1) == 1, y_index >= 2
        embeddings = jnp.concatenate([here_ref[...], beside_ref[...]], axis=0)
        parts = []
        for line_ref, out_ref in ((own_ref, own_out), (other_ref, other_out)):
            line = line_ref[...]
            quarter = line.shape[1] // 4
            dots = [
                dot_rows(
                    embeddings[:, k * quarter : (k + 1) * quarter],
                    line[:, k * quarter : (k + 1) * quarter],
                )
                for k in range(4)
            ]
            exps = jnp.exp((dots[0] + dots[1] + dots[2] + dots[3]) * inv_temp)
            out_ref[:passes] = jnp.where(odd, exps[passes:], exps[:passes])
            out_ref[passes:] = jnp.where(odd, exps[:passes], exps[passes:])
            parts.append(jnp.sum(exps, axis=0, keepdims=True))
        first = jnp.where(high, parts[1], parts[0])
        second = jnp.where(high, parts[0], parts[1])
        row = lax.broadcasted_iota(jnp.int32, (2, queries), 0)
        both = jnp.where(row == 0, first, second)
        sums_out[...] = jnp.broadcast_to(both[None], sums_out.shape)

    vmem = pl.BlockSpec(memory_space=pltpu.VMEM)
    exps = jax.ShapeDtypeStruct((2 * passes, queries), jnp.float32)
    return pl.pallas_call(
        kernel,
        out_shape=(exps, exps, jax.ShapeDtypeStruct((count, 2, queries), jnp.float32)),
        in_specs=[vmem] * 4,
        out_specs=(vmem, vmem, vmem),
        compiler_params=pltpu.CompilerParams(vmem_limit_bytes=16 << 20),
        name="score",
    )(*embeds, own_line, other_line)


def gradients(own_exp, other_exp, part_totals, own_line, other_line, own_at, other_at, factor):
    passes, queries = own_exp.shape
    width = own_line.shape[1] // S

    def kernel(
        own_exp_ref, other_exp_ref, totals_ref, own_ref, other_ref, own_at_ref, other_at_ref, out_ref
    ):
        dp_index = lax.axis_index("dp")
        high = (dp_index & (Y - 1)) >= 2
        totals = jnp.sum(totals_ref[...], axis=0)
        low_total, high_total = totals[0:1], totals[1:2]
        passage = lax.broadcasted_iota(jnp.int32, (passes, queries), 0)
        passage += (dp_index - (dp_index & 1)) * (passes // 2)

        def coefficients(exp_ref, total, at_ref):
            target = (passage == at_ref[...]).astype(jnp.float32)
            return ((exp_ref[...] / total - target) * factor).astype(jnp.bfloat16)

        own = coefficients(own_exp_ref, jnp.where(high, high_total, low_total), own_at_ref)
        other = coefficients(other_exp_ref, jnp.where(high, low_total, high_total), other_at_ref)
        for part in range(S):
            columns = pl.ds(part * width, width)
            block = jnp.dot(
                own, own_ref[:, columns], preferred_element_type=jnp.float32
            ) + jnp.dot(other, other_ref[:, columns], preferred_element_type=jnp.float32)
            block = block.astype(jnp.bfloat16)
            out_ref[part] = block[: passes // 2]
            out_ref[S + part] = block[passes // 2 :]

    vmem = pl.BlockSpec(memory_space=pltpu.VMEM)
    return pl.pallas_call(
        kernel,
        out_shape=jax.ShapeDtypeStruct((2 * S, passes // 2, width), jnp.bfloat16),
        in_specs=[vmem] * 7,
        out_specs=vmem,
        compiler_params=pltpu.CompilerParams(vmem_limit_bytes=16 << 20),
        name="gradients",
    )(own_exp, other_exp, part_totals, own_line, other_line, own_at, other_at)


def swap_seq(block, mask):
    return lax.ppermute(block, "seq", [(i, i ^ mask) for i in range(S)])


def swap_y(block, mask):
    return lax.ppermute(block, "dp", [(i, i ^ mask) for i in range(Z * Y)])


def per_device(token_rows, extra_len, queries, positive):
    row_count, width = token_rows.shape
    pass_count = extra_len.shape[1]
    own = queries.shape[0]
    seq_index = lax.axis_index("seq")
    dp_index = lax.axis_index("dp")
    y_index = dp_index & (Y - 1)

    lengths = extra_len[0] + 15
    lengths, queries = lax.optimization_barrier((lengths, queries))
    copies = normalized_copies(queries, Z)
    own_line = lax.all_to_all(copies, "dp", 0, 0, axis_index_groups=Z_GROUPS)
    by_line = jnp.roll(positive.reshape(Z, Y, S, own), -FIRST, axis=0)

    def line_positive(y):
        return lax.dynamic_slice(by_line, (0, y, seq_index, 0), (Z, 1, 1, own)).reshape(-1)

    upto = jnp.tril(jnp.ones((pass_count, pass_count), jnp.int32))
    end_rows = jnp.sum(upto * lengths[None, :], axis=1)
    first_rows = end_rows - lengths
    row_pos = seq_index * row_count + jnp.arange(row_count, dtype=jnp.int32)
    member = (
        (row_pos[None, :] >= first_rows[:, None]) & (row_pos[None, :] < end_rows[:, None])
    ).astype(jnp.bfloat16)
    sums = jnp.dot(member, token_rows, preferred_element_type=jnp.float32)

    def over_seq(step, sums):
        for mask in (1, 2, 6):
            sums = sums + swap_seq(sums.astype(jnp.bfloat16), mask).astype(jnp.float32)
        return sums

    sums = lax.fori_loop(0, jnp.minimum(lengths[0], 1), over_seq, sums)
    float_len = lengths.astype(jnp.float32)[:, None]
    pooled = sums / float_len
    inv_norm = lax.rsqrt(jnp.sum(pooled * pooled, axis=-1, keepdims=True) + 1e-06)
    embedding = pooled * inv_norm

    embed_half, own_line = lax.optimization_barrier((embedding.astype(jnp.bfloat16), own_line))
    own_line, other_line, beside = lax.optimization_barrier(
        (own_line, swap_y(own_line, 3), swap_y(embed_half, 1))
    )
    own_line = own_line.reshape(Z * own, width)
    other_line = other_line.reshape(Z * own, width)
    own_exp, other_exp, parts = score((embed_half, beside), own_line, other_line, 2 * Z)
    part_totals = lax.all_to_all(parts, "dp", 0, 0, axis_index_groups=LINES)

    d_partial = gradients(
        own_exp,
        other_exp,
        part_totals,
        own_line,
        other_line,
        line_positive(y_index)[None, :],
        line_positive(3 - y_index)[None, :],
        loss_scale * inv_temp / positive.shape[0],
    )
    d_parts = lax.all_to_all(d_partial, ("dp", "seq"), 0, 0, axis_index_groups=PAIRS)
    d_own = jnp.sum(d_parts.astype(jnp.float32), axis=0).astype(jnp.bfloat16)
    d_embed = share(d_own, "seq", S).transpose(1, 0, 2).reshape(pass_count, width)
    d_embed = d_embed.astype(jnp.float32)
    d_pooled = inv_norm * (
        d_embed - embedding * jnp.sum(embedding * d_embed, axis=-1, keepdims=True)
    )
    every_d_sum = (d_pooled / float_len).astype(jnp.bfloat16)
    grads = lax.dot_general(
        member, every_d_sum, (((0,), (0,)), ((), ())), preferred_element_type=jnp.float32
    )
    return grads.astype(jnp.bfloat16)


def solution(mesh):
    return jax.shard_map(
        per_device,
        mesh=mesh,
        in_specs=(P(("dp", "seq"), None), P("dp", None), P(("dp", "seq"), None), P()),
        out_specs=P(("dp", "seq"), None),
        check_vma=False,
    )
```

```python
import jax
import jax.numpy as jnp
from jax import lax
from jax.experimental import pallas as pl
from jax.experimental.pallas import tpu as pltpu
from jax.sharding import PartitionSpec as P

loss_scale = 1048576.0
inv_temp = 20.0
Z, Y, S = 16, 4, 8
FIRST, SECOND = 14, 8
Z_GROUPS = [[(z + FIRST) % Z * Y + y for z in range(Z)] for y in range(Y)]
SEQ = [(s + 4) % S for s in range(S)]
PAIRS = [[(2 * p + i) * S + s for i in range(2) for s in SEQ] for p in range(Z * Y // 2)]
LINES = [
    [(z + SECOND) % Z * Y + y for z in range(Z) for y in (low, 3 - low)] for low in range(2)
]


def share(block, axis, count, groups=None):
    copies = jnp.broadcast_to(block[None], (count,) + block.shape)
    return lax.all_to_all(copies, axis, 0, 0, axis_index_groups=groups)


def normalized_copies(queries, count):
    def kernel(in_ref, out_ref):
        query = in_ref[...].astype(jnp.float32)
        scale = lax.rsqrt(jnp.sum(query * query, axis=-1, keepdims=True) + 1e-06)
        rounded = (query * scale).astype(jnp.bfloat16)
        for i in range(count):
            out_ref[i] = rounded

    return pl.pallas_call(
        kernel,
        out_shape=jax.ShapeDtypeStruct((count,) + queries.shape, jnp.bfloat16),
        in_specs=[pl.BlockSpec(memory_space=pltpu.VMEM)],
        out_specs=pl.BlockSpec(memory_space=pltpu.VMEM),
        compiler_params=pltpu.CompilerParams(vmem_limit_bytes=8 << 20),
        name="normalized_copies",
    )(queries)


def dot_rows(left, right):
    return lax.dot_general(
        left, right, (((1,), (1,)), ((), ())), preferred_element_type=jnp.float32
    )


def score(embeds, own_line, other_line, count):
    passes, queries = embeds[0].shape[0], own_line.shape[0]

    def kernel(here_ref, beside_ref, own_ref, other_ref, own_out, other_out, sums_out):
        y_index = lax.axis_index("dp") & (Y - 1)
        odd, high = (y_index & 1) == 1, y_index >= 2
        embeddings = jnp.concatenate([here_ref[...], beside_ref[...]], axis=0)
        parts = []
        for line_ref, out_ref in ((own_ref, own_out), (other_ref, other_out)):
            line = line_ref[...]
            quarter = line.shape[1] // 4
            dots = [
                dot_rows(
                    embeddings[:, k * quarter : (k + 1) * quarter],
                    line[:, k * quarter : (k + 1) * quarter],
                )
                for k in range(4)
            ]
            exps = jnp.exp((dots[0] + dots[1] + dots[2] + dots[3]) * inv_temp)
            out_ref[:passes] = jnp.where(odd, exps[passes:], exps[:passes])
            out_ref[passes:] = jnp.where(odd, exps[:passes], exps[passes:])
            parts.append(jnp.sum(exps, axis=0, keepdims=True))
        first = jnp.where(high, parts[1], parts[0])
        second = jnp.where(high, parts[0], parts[1])
        row = lax.broadcasted_iota(jnp.int32, (2, queries), 0)
        both = jnp.where(row == 0, first, second)
        sums_out[...] = jnp.broadcast_to(both[None], sums_out.shape)

    vmem = pl.BlockSpec(memory_space=pltpu.VMEM)
    exps = jax.ShapeDtypeStruct((2 * passes, queries), jnp.float32)
    return pl.pallas_call(
        kernel,
        out_shape=(exps, exps, jax.ShapeDtypeStruct((count, 2, queries), jnp.float32)),
        in_specs=[vmem] * 4,
        out_specs=(vmem, vmem, vmem),
        compiler_params=pltpu.CompilerParams(vmem_limit_bytes=16 << 20),
        name="score",
    )(*embeds, own_line, other_line)


def gradients(own_exp, other_exp, part_totals, own_line, other_line, own_at, other_at, factor):
    passes, queries = own_exp.shape
    width = own_line.shape[1] // S

    def kernel(
        own_exp_ref, other_exp_ref, totals_ref, own_ref, other_ref, own_at_ref, other_at_ref, out_ref
    ):
        dp_index = lax.axis_index("dp")
        high = (dp_index & (Y - 1)) >= 2
        totals = jnp.sum(totals_ref[...], axis=0)
        low_total, high_total = totals[0:1], totals[1:2]
        passage = lax.broadcasted_iota(jnp.int32, (passes, queries), 0)
        passage += (dp_index - (dp_index & 1)) * (passes // 2)

        def coefficients(exp_ref, total, at_ref):
            target = (passage == at_ref[...]).astype(jnp.float32)
            return ((exp_ref[...] / total - target) * factor).astype(jnp.bfloat16)

        own = coefficients(own_exp_ref, jnp.where(high, high_total, low_total), own_at_ref)
        other = coefficients(other_exp_ref, jnp.where(high, low_total, high_total), other_at_ref)
        for part in range(S):
            columns = pl.ds(part * width, width)
            block = jnp.dot(
                own, own_ref[:, columns], preferred_element_type=jnp.float32
            ) + jnp.dot(other, other_ref[:, columns], preferred_element_type=jnp.float32)
            block = block.astype(jnp.bfloat16)
            out_ref[part] = block[: passes // 2]
            out_ref[S + part] = block[passes // 2 :]

    vmem = pl.BlockSpec(memory_space=pltpu.VMEM)
    return pl.pallas_call(
        kernel,
        out_shape=jax.ShapeDtypeStruct((2 * S, passes // 2, width), jnp.bfloat16),
        in_specs=[vmem] * 7,
        out_specs=vmem,
        compiler_params=pltpu.CompilerParams(vmem_limit_bytes=16 << 20),
        name="gradients",
    )(own_exp, other_exp, part_totals, own_line, other_line, own_at, other_at)


def swap_seq(block, mask):
    return lax.ppermute(block, "seq", [(i, i ^ mask) for i in range(S)])


def swap_y(block, mask):
    return lax.ppermute(block, "dp", [(i, i ^ mask) for i in range(Z * Y)])


def per_device(token_rows, extra_len, queries, positive):
    row_count, width = token_rows.shape
    pass_count = extra_len.shape[1]
    own = queries.shape[0]
    seq_index = lax.axis_index("seq")
    dp_index = lax.axis_index("dp")
    y_index = dp_index & (Y - 1)

    lengths = extra_len[0] + 15
    lengths, queries = lax.optimization_barrier((lengths, queries))
    copies = normalized_copies(queries, Z)
    own_line = lax.all_to_all(copies, "dp", 0, 0, axis_index_groups=Z_GROUPS)
    by_line = jnp.roll(positive.reshape(Z, Y, S, own), -FIRST, axis=0)

    def line_positive(y):
        return lax.dynamic_slice(by_line, (0, y, seq_index, 0), (Z, 1, 1, own)).reshape(-1)

    upto = jnp.tril(jnp.ones((pass_count, pass_count), jnp.int32))
    end_rows = jnp.sum(upto * lengths[None, :], axis=1)
    first_rows = end_rows - lengths
    row_pos = seq_index * row_count + jnp.arange(row_count, dtype=jnp.int32)
    member = (
        (row_pos[None, :] >= first_rows[:, None]) & (row_pos[None, :] < end_rows[:, None])
    ).astype(jnp.bfloat16)
    sums = jnp.dot(member, token_rows, preferred_element_type=jnp.float32)

    def over_seq(step, sums):
        for mask in (1, 2, 6):
            sums = sums + swap_seq(sums.astype(jnp.bfloat16), mask).astype(jnp.float32)
        return sums

    sums = lax.fori_loop(0, jnp.minimum(lengths[0], 1), over_seq, sums)
    float_len = lengths.astype(jnp.float32)[:, None]
    pooled = sums / float_len
    inv_norm = lax.rsqrt(jnp.sum(pooled * pooled, axis=-1, keepdims=True) + 1e-06)
    embedding = pooled * inv_norm

    embed_half, own_line = lax.optimization_barrier((embedding.astype(jnp.bfloat16), own_line))
    own_line, other_line, beside = lax.optimization_barrier(
        (own_line, swap_y(own_line, 3), swap_y(embed_half, 1))
    )
    own_line = own_line.reshape(Z * own, width)
    other_line = other_line.reshape(Z * own, width)
    own_exp, other_exp, parts = score((embed_half, beside), own_line, other_line, 2 * Z)
    part_totals = lax.all_to_all(parts, "dp", 0, 0, axis_index_groups=LINES)

    d_partial = gradients(
        own_exp,
        other_exp,
        part_totals,
        own_line,
        other_line,
        line_positive(y_index)[None, :],
        line_positive(3 - y_index)[None, :],
        loss_scale * inv_temp / positive.shape[0],
    )
    d_parts = lax.all_to_all(d_partial, ("dp", "seq"), 0, 0, axis_index_groups=PAIRS)
    d_own = jnp.sum(d_parts.astype(jnp.float32), axis=0).astype(jnp.bfloat16)
    d_embed = share(d_own, "seq", S, [SEQ]).transpose(1, 0, 2).reshape(pass_count, width)
    d_embed = d_embed.astype(jnp.float32)
    d_pooled = inv_norm * (
        d_embed - embedding * jnp.sum(embedding * d_embed, axis=-1, keepdims=True)
    )
    every_d_sum = (d_pooled / float_len).astype(jnp.bfloat16)
    grads = lax.dot_general(
        member, every_d_sum, (((0,), (0,)), ((), ())), preferred_element_type=jnp.float32
    )
    return grads.astype(jnp.bfloat16)


def solution(mesh):
    return jax.shard_map(
        per_device,
        mesh=mesh,
        in_specs=(P(("dp", "seq"), None), P("dp", None), P(("dp", "seq"), None), P()),
        out_specs=P(("dp", "seq"), None),
        check_vma=False,
    )
```

```python
import jax
import jax.numpy as jnp
from jax import lax
from jax.experimental import pallas as pl
from jax.experimental.pallas import tpu as pltpu
from jax.sharding import PartitionSpec as P

loss_scale = 1048576.0
inv_temp = 20.0
Z, Y, S = 16, 4, 8
FIRST, SECOND = 14, 8
Z_GROUPS = [[(z + FIRST) % Z * Y + y for z in range(Z)] for y in range(Y)]
SEQ = [(s + 4) % S for s in range(S)]
PAIRS = [[(2 * p + i) * S + s for i in range(2) for s in SEQ] for p in range(Z * Y // 2)]
LINES = [
    [(z + SECOND) % Z * Y + y for z in range(Z) for y in (3 - low, low)] for low in range(2)
]


def share(block, axis, count, groups=None):
    copies = jnp.broadcast_to(block[None], (count,) + block.shape)
    return lax.all_to_all(copies, axis, 0, 0, axis_index_groups=groups)


def normalized_copies(queries, count):
    def kernel(in_ref, out_ref):
        query = in_ref[...].astype(jnp.float32)
        scale = lax.rsqrt(jnp.sum(query * query, axis=-1, keepdims=True) + 1e-06)
        rounded = (query * scale).astype(jnp.bfloat16)
        for i in range(count):
            out_ref[i] = rounded

    return pl.pallas_call(
        kernel,
        out_shape=jax.ShapeDtypeStruct((count,) + queries.shape, jnp.bfloat16),
        in_specs=[pl.BlockSpec(memory_space=pltpu.VMEM)],
        out_specs=pl.BlockSpec(memory_space=pltpu.VMEM),
        compiler_params=pltpu.CompilerParams(vmem_limit_bytes=8 << 20),
        name="normalized_copies",
    )(queries)


def dot_rows(left, right):
    return lax.dot_general(
        left, right, (((1,), (1,)), ((), ())), preferred_element_type=jnp.float32
    )


def score(embeds, own_line, other_line, count):
    passes, queries = embeds[0].shape[0], own_line.shape[0]

    def kernel(here_ref, beside_ref, own_ref, other_ref, own_out, other_out, sums_out):
        y_index = lax.axis_index("dp") & (Y - 1)
        odd, high = (y_index & 1) == 1, y_index >= 2
        embeddings = jnp.concatenate([here_ref[...], beside_ref[...]], axis=0)
        parts = []
        for line_ref, out_ref in ((own_ref, own_out), (other_ref, other_out)):
            line = line_ref[...]
            quarter = line.shape[1] // 4
            dots = [
                dot_rows(
                    embeddings[:, k * quarter : (k + 1) * quarter],
                    line[:, k * quarter : (k + 1) * quarter],
                )
                for k in range(4)
            ]
            exps = jnp.exp((dots[0] + dots[1] + dots[2] + dots[3]) * inv_temp)
            out_ref[:passes] = jnp.where(odd, exps[passes:], exps[:passes])
            out_ref[passes:] = jnp.where(odd, exps[:passes], exps[passes:])
            parts.append(jnp.sum(exps, axis=0, keepdims=True))
        first = jnp.where(high, parts[1], parts[0])
        second = jnp.where(high, parts[0], parts[1])
        row = lax.broadcasted_iota(jnp.int32, (2, queries), 0)
        both = jnp.where(row == 0, first, second)
        sums_out[...] = jnp.broadcast_to(both[None], sums_out.shape)

    vmem = pl.BlockSpec(memory_space=pltpu.VMEM)
    exps = jax.ShapeDtypeStruct((2 * passes, queries), jnp.float32)
    return pl.pallas_call(
        kernel,
        out_shape=(exps, exps, jax.ShapeDtypeStruct((count, 2, queries), jnp.float32)),
        in_specs=[vmem] * 4,
        out_specs=(vmem, vmem, vmem),
        compiler_params=pltpu.CompilerParams(vmem_limit_bytes=16 << 20),
        name="score",
    )(*embeds, own_line, other_line)


def gradients(own_exp, other_exp, part_totals, own_line, other_line, own_at, other_at, factor):
    passes, queries = own_exp.shape
    width = own_line.shape[1] // S

    def kernel(
        own_exp_ref, other_exp_ref, totals_ref, own_ref, other_ref, own_at_ref, other_at_ref, out_ref
    ):
        dp_index = lax.axis_index("dp")
        high = (dp_index & (Y - 1)) >= 2
        totals = jnp.sum(totals_ref[...], axis=0)
        low_total, high_total = totals[0:1], totals[1:2]
        passage = lax.broadcasted_iota(jnp.int32, (passes, queries), 0)
        passage += (dp_index - (dp_index & 1)) * (passes // 2)

        def coefficients(exp_ref, total, at_ref):
            target = (passage == at_ref[...]).astype(jnp.float32)
            return ((exp_ref[...] / total - target) * factor).astype(jnp.bfloat16)

        own = coefficients(own_exp_ref, jnp.where(high, high_total, low_total), own_at_ref)
        other = coefficients(other_exp_ref, jnp.where(high, low_total, high_total), other_at_ref)
        for part in range(S):
            columns = pl.ds(part * width, width)
            block = jnp.dot(
                own, own_ref[:, columns], preferred_element_type=jnp.float32
            ) + jnp.dot(other, other_ref[:, columns], preferred_element_type=jnp.float32)
            block = block.astype(jnp.bfloat16)
            out_ref[part] = block[: passes // 2]
            out_ref[S + part] = block[passes // 2 :]

    vmem = pl.BlockSpec(memory_space=pltpu.VMEM)
    return pl.pallas_call(
        kernel,
        out_shape=jax.ShapeDtypeStruct((2 * S, passes // 2, width), jnp.bfloat16),
        in_specs=[vmem] * 7,
        out_specs=vmem,
        compiler_params=pltpu.CompilerParams(vmem_limit_bytes=16 << 20),
        name="gradients",
    )(own_exp, other_exp, part_totals, own_line, other_line, own_at, other_at)


def swap_seq(block, mask):
    return lax.ppermute(block, "seq", [(i, i ^ mask) for i in range(S)])


def swap_y(block, mask):
    return lax.ppermute(block, "dp", [(i, i ^ mask) for i in range(Z * Y)])


def per_device(token_rows, extra_len, queries, positive):
    row_count, width = token_rows.shape
    pass_count = extra_len.shape[1]
    own = queries.shape[0]
    seq_index = lax.axis_index("seq")
    dp_index = lax.axis_index("dp")
    y_index = dp_index & (Y - 1)

    lengths = extra_len[0] + 15
    lengths, queries = lax.optimization_barrier((lengths, queries))
    copies = normalized_copies(queries, Z)
    own_line = lax.all_to_all(copies, "dp", 0, 0, axis_index_groups=Z_GROUPS)
    by_line = jnp.roll(positive.reshape(Z, Y, S, own), -FIRST, axis=0)

    def line_positive(y):
        return lax.dynamic_slice(by_line, (0, y, seq_index, 0), (Z, 1, 1, own)).reshape(-1)

    upto = jnp.tril(jnp.ones((pass_count, pass_count), jnp.int32))
    end_rows = jnp.sum(upto * lengths[None, :], axis=1)
    first_rows = end_rows - lengths
    row_pos = seq_index * row_count + jnp.arange(row_count, dtype=jnp.int32)
    member = (
        (row_pos[None, :] >= first_rows[:, None]) & (row_pos[None, :] < end_rows[:, None])
    ).astype(jnp.bfloat16)
    sums = jnp.dot(member, token_rows, preferred_element_type=jnp.float32)

    def over_seq(step, sums):
        for mask in (1, 2, 6):
            sums = sums + swap_seq(sums.astype(jnp.bfloat16), mask).astype(jnp.float32)
        return sums

    sums = lax.fori_loop(0, jnp.minimum(lengths[0], 1), over_seq, sums)
    float_len = lengths.astype(jnp.float32)[:, None]
    pooled = sums / float_len
    inv_norm = lax.rsqrt(jnp.sum(pooled * pooled, axis=-1, keepdims=True) + 1e-06)
    embedding = pooled * inv_norm

    embed_half, own_line = lax.optimization_barrier((embedding.astype(jnp.bfloat16), own_line))
    own_line, other_line, beside = lax.optimization_barrier(
        (own_line, swap_y(own_line, 3), swap_y(embed_half, 1))
    )
    own_line = own_line.reshape(Z * own, width)
    other_line = other_line.reshape(Z * own, width)
    own_exp, other_exp, parts = score((embed_half, beside), own_line, other_line, 2 * Z)
    part_totals = lax.all_to_all(parts, "dp", 0, 0, axis_index_groups=LINES)

    d_partial = gradients(
        own_exp,
        other_exp,
        part_totals,
        own_line,
        other_line,
        line_positive(y_index)[None, :],
        line_positive(3 - y_index)[None, :],
        loss_scale * inv_temp / positive.shape[0],
    )
    d_parts = lax.all_to_all(d_partial, ("dp", "seq"), 0, 0, axis_index_groups=PAIRS)
    d_own = jnp.sum(d_parts.astype(jnp.float32), axis=0).astype(jnp.bfloat16)
    d_embed = share(d_own, "seq", S, [SEQ]).transpose(1, 0, 2).reshape(pass_count, width)
    d_embed = d_embed.astype(jnp.float32)
    d_pooled = inv_norm * (
        d_embed - embedding * jnp.sum(embedding * d_embed, axis=-1, keepdims=True)
    )
    every_d_sum = (d_pooled / float_len).astype(jnp.bfloat16)
    grads = lax.dot_general(
        member, every_d_sum, (((0,), (0,)), ((), ())), preferred_element_type=jnp.float32
    )
    return grads.astype(jnp.bfloat16)


def solution(mesh):
    return jax.shard_map(
        per_device,
        mesh=mesh,
        in_specs=(P(("dp", "seq"), None), P("dp", None), P(("dp", "seq"), None), P()),
        out_specs=P(("dp", "seq"), None),
        check_vma=False,
    )
```
